32 devices in a mesh: seq: 16 (over z, x, core), chan: 2 (over y).
Axes of the slice: x: 2, y: 2, z: 4, core: 2. Of those that a mesh axis runs over, the one named last changes fastest.
Arguments:
- query_in: bfloat16 [8192, 4096], P('seq', 'chan'), may hold values from -6 to 6
- key_in: bfloat16 [8192, 4096], P('seq', 'chan'), may hold values from -6 to 6
- value_in: bfloat16 [8192, 4096], P('seq', 'chan'), may hold values from -6 to 6
- short_weight: float32 [3, 3, 4096], P(None, None, 'chan'), may hold values from -3.5 to 3.5
- long_filter: float32 [256, 8192], P('chan', 'seq'), may hold values from 0 to 0.5
- skip_gain: float32 [4096], P('chan'), may hold values from 0.5 to 1.5
- w_out: bfloat16 [4096, 8192], P('chan', 'seq'), may hold values from -0.125 to 0.125
Outputs:
- mixer_out: bfloat16 [8192, 8192], P('seq', 'chan')
The draws below stay inside these ranges and needn't reach their ends.
All inputs are finite; a program needn't handle non-finite values.
Results may differ from the reference program's by a relative error of at most 0.018.
Values may be sent and summed in bfloat16 or wider, within the bound.
A program may use at most 192 MiB of HBM per device.

```python
import jax
import jax.numpy as jnp
from jax import lax

D = 8192
DW = 4096
GROUP = 16
KW = 3
LENGTH = 8192
GROUPS = 256
N_CHAN = 2


def draw_long_filter(key, part):
    keys = jax.random.split(key, 6)
    lag_int = jnp.arange(LENGTH, dtype=jnp.int32)
    lag_pos = lag_int.astype(jnp.float32)
    slow_reach = jnp.exp(jax.random.uniform(keys[0], (GROUPS,), jnp.float32, jnp.log(LENGTH * 0.5), jnp.log(LENGTH * 8.0)))
    fast_reach = jax.random.uniform(keys[1], (GROUPS,), jnp.float32, 30.0, 50.0)
    fast = jax.random.randint(keys[2], (GROUPS,), 0, 2) == 0
    rough = jax.random.uniform(keys[3], (GROUPS, LENGTH), jnp.float32, 0.5, 1.5)
    reach = jnp.where(fast, fast_reach, slow_reach)
    spots = jax.random.randint(keys[4], (GROUPS, 3), 0, LENGTH)
    drops = jnp.log(jax.random.uniform(keys[5], (GROUPS, 3), jnp.float32, 0.5, 0.8))
    fallen = jnp.sum(jnp.where(lag_int[None, None, :] >= spots[:, :, None], drops[:, :, None], 0.0), axis=1)
    height = jnp.sqrt(2.0 / jnp.minimum(reach, LENGTH * 1.0))
    return height[:, None] * jnp.exp(-lag_pos[None, :] / reach[:, None] + fallen) * rough


def spiked(drawn, stream_key, source, target, shards_of, factor):
    owner, partner = [(jnp.arange(drawn.shape[axis_at]) // (drawn.shape[axis_at] // shards_of)).reshape([-1 if axis == axis_at else 1 for axis in range(drawn.ndim)]) for axis_at in (source, target)]
    chosen = jax.random.permutation(stream_key, shards_of)[partner]
    strong = (owner == chosen) | (owner == (partner + shards_of // 2) % shards_of)
    return jnp.where(strong, factor * drawn, drawn)


def shard_levels(own_key, dims, shards, smallest, high):
    level = 1.0
    for dim, parts in shards:
        steps = jax.random.uniform(jax.random.fold_in(jax.random.fold_in(own_key, 6), dim), (parts,), jnp.float32, smallest / len(shards), high / len(shards))
        level = level * jnp.repeat(jnp.exp(steps), dims[dim] // parts).reshape((-1,) + (1,) * (len(dims) - 1 - dim))
    return level


def centred(rng, dims, spread, bound, shards=(), kind=jnp.bfloat16):
    values = spread * jax.random.normal(rng, dims, jnp.float32)
    if shards:
        values = values * shard_levels(rng, dims, shards, -0.22, 0.18)
    return jnp.clip(values, -bound, bound).astype(kind)


def bell_draw_with(own_key, dims, spread, most, cuts, heavy, held_as=jnp.bfloat16):
    entries = spread * jax.random.normal(own_key, dims, jnp.float32)
    if cuts:
        entries = entries * shard_levels(own_key, dims, cuts, -0.22, 0.18)
    return jnp.clip(spiked(entries, jax.random.fold_in(own_key, 3), *heavy), -most, most).astype(held_as)


def setup_inputs(seed: int = 0) -> dict:
    splits = jax.random.split(jax.random.key(seed), 8)
    query_in = centred(splits[0], (LENGTH, DW), 1.0, 6.0, ((0, 16), (1, 2)))
    key_in = centred(splits[1], (LENGTH, DW), 1.0, 6.0, ((0, 16), (1, 2)))
    value_in = centred(splits[2], (LENGTH, DW), 1.0, 6.0, ((0, 16), (1, 2)))
    short_weight = centred(splits[3], (3, KW, DW), KW ** -0.5, 3.5, ((2, 2),), jnp.float32)
    long_filter = draw_long_filter(jax.random.fold_in(splits[7], 71), 0)
    skip_gain = jnp.clip(0.5 + 1.0 * jax.random.uniform(splits[5], (DW,), jnp.float32) ** shard_levels(splits[5], (DW,), ((0, 2),), -0.2, 0.2), 0.5, 1.5)
    w_out = bell_draw_with(splits[6], (DW, D), DW ** -0.5, 0.125, ((0, 2), (1, 16)), (0, 1, 16, 2.0))
    return dict(query_in=query_in, key_in=key_in, value_in=value_in, short_weight=short_weight, long_filter=long_filter, skip_gain=skip_gain, w_out=w_out)


def short_conv(signal, taps):
    padded = jnp.pad(signal.astype(jnp.float32), ((KW - 1, 0), (0, 0)))
    summed = taps[0] * padded[KW - 1: KW - 1 + LENGTH]
    for shift in range(1, KW):
        summed = summed + taps[shift] * padded[KW - 1 - shift: KW - 1 - shift + LENGTH]
    return summed


def group_conv(operands):
    block, filt_row = operands
    spectrum = jnp.fft.rfft(block.astype(jnp.float32), n=2 * LENGTH, axis=0)
    kernel = jnp.fft.rfft(filt_row, n=2 * LENGTH)
    result = jnp.fft.irfft(spectrum * kernel[:, None], n=2 * LENGTH, axis=0)[:LENGTH]
    return result.astype(jnp.bfloat16)


def reference(query_in, key_in, value_in, short_weight, long_filter, skip_gain, w_out):
    query_conv = short_conv(query_in, short_weight[0]).astype(jnp.bfloat16)
    key_conv = short_conv(key_in, short_weight[1])
    value_conv = short_conv(value_in, short_weight[2])
    gated = (key_conv * value_conv).astype(jnp.bfloat16)
    grouped = gated.reshape(LENGTH, GROUPS, GROUP).transpose(1, 0, 2)
    convs = lax.map(group_conv, (grouped, long_filter))
    conv = convs.transpose(1, 0, 2).reshape(LENGTH, DW)
    mixed = (query_conv.astype(jnp.float32) * (conv.astype(jnp.float32) + skip_gain * gated.astype(jnp.float32))).astype(jnp.bfloat16)
    slab = DW // N_CHAN
    summed = jnp.zeros((LENGTH, D), jnp.float32)
    for member in range(N_CHAN):
        first = member * slab
        partial_value = jnp.dot(mixed[:, first:first + slab], w_out[first:first + slab], preferred_element_type=jnp.float32)
        summed = summed + lax.optimization_barrier(partial_value.astype(jnp.bfloat16)).astype(jnp.float32)
    return summed.astype(jnp.bfloat16)
```

```python
import functools

import jax
import jax.numpy as jnp
from jax import lax
from jax.experimental import pallas as pl
from jax.experimental.pallas import tpu as pltpu
from jax.sharding import PartitionSpec as P

GROUP = 16
KW = 3
BLOCK = 256
TILE = 128


def short_taps(x, border, taps):
    rows = x.shape[0]
    extended = jnp.concatenate([border, x.astype(jnp.float32)], axis=0)
    first = border.shape[0]
    total = taps[0:1] * extended[first:]
    for shift in range(1, KW):
        total = total + taps[shift : shift + 1] * extended[first - shift : first - shift + rows]
    return total


def front_kernel(q_ref, k_ref, v_ref, border_ref, taps_ref, query_ref, gated_ref):
    query = short_taps(q_ref[...], border_ref[0], taps_ref[0])
    key = short_taps(k_ref[...], border_ref[1], taps_ref[1])
    value = short_taps(v_ref[...], border_ref[2], taps_ref[2])
    query_ref[...] = query.T.astype(jnp.bfloat16)
    gated_ref[...] = (key * value).T.astype(jnp.bfloat16)


def front(query_in, key_in, value_in, border, taps):
    rows, width = query_in.shape
    wide = min(width, 256)
    signal = pl.BlockSpec((rows, wide), lambda i: (0, i))
    turned = pl.BlockSpec((wide, rows), lambda i: (i, 0))
    return pl.pallas_call(
        front_kernel,
        grid=(width // wide,),
        in_specs=[
            signal,
            signal,
            signal,
            pl.BlockSpec((3, 8, wide), lambda i: (0, 0, i)),
            pl.BlockSpec((3, KW, wide), lambda i: (0, 0, i)),
        ],
        out_specs=[turned, turned],
        out_shape=[jax.ShapeDtypeStruct((width, rows), jnp.bfloat16)] * 2,
        compiler_params=pltpu.CompilerParams(vmem_limit_bytes=32 * 1024 * 1024),
        cost_estimate=pl.CostEstimate(
            flops=20 * rows * width, bytes_accessed=10 * rows * width, transcendentals=0
        ),
    )(query_in, key_in, value_in, border, taps)


def conv_kernel(parts, blocks, data_ref, lags_ref, out_ref, held, toeplitz, total):
    local_len = data_ref.shape[2]
    per = local_len // BLOCK
    rows = blocks * GROUP
    held[0:rows, :] = jnp.zeros((rows, BLOCK), held.dtype)
    for part in range(parts):
        for piece in range(per):
            at = rows + (part * per + piece) * GROUP
            held[at : at + GROUP, :] = data_ref[part, :, piece * BLOCK : (piece + 1) * BLOCK]

    tiles = toeplitz.shape[0]

    def build(m, carry):
        line = jnp.broadcast_to(lags_ref[0, pl.ds(m, 1), :], (TILE, 2 * TILE))
        turned = pltpu.roll(line, 0, 1, stride=1, stride_axis=0)
        toeplitz[pl.ds(m, 1)] = turned[:, TILE:].astype(jnp.bfloat16)[None]
        return carry

    lax.fori_loop(0, tiles, build, 0)
    total[...] = jnp.zeros_like(total)
    half = rows // 2

    def weights(k):
        now = toeplitz[2 * k + 1]
        return jnp.concatenate(
            [
                jnp.concatenate([now, toeplitz[2 * k + 2]], axis=1),
                jnp.concatenate([toeplitz[2 * k], now], axis=1),
            ],
            axis=0,
        )

    def near(k, carry):
        start = pl.multiple_of(rows - k * GROUP, GROUP)
        total[...] += jnp.dot(
            held[pl.ds(start, rows), :], weights(k), preferred_element_type=jnp.float32
        )
        return carry

    def far(k, carry):
        start = pl.multiple_of(rows + half - k * GROUP, GROUP)
        total[half:, :] += jnp.dot(
            held[pl.ds(start, half), :], weights(k), preferred_element_type=jnp.float32
        )
        return carry

    lax.fori_loop(0, blocks // 2, near, 0)
    lax.fori_loop(blocks // 2, blocks, far, 0)
    for part in range(parts):
        for piece in range(per):
            at = (part * per + piece) * GROUP
            out_ref[part, :, piece * BLOCK : (piece + 1) * BLOCK] = total[
                at : at + GROUP, :
            ].astype(jnp.bfloat16)


def long_conv(data, lags):
    parts, channels, local_len = data.shape
    groups, tiles, _ = lags.shape
    blocks = parts * local_len // BLOCK
    rows = blocks * GROUP
    return pl.pallas_call(
        functools.partial(conv_kernel, parts, blocks),
        grid=(groups,),
        in_specs=[
            pl.BlockSpec((parts, GROUP, local_len), lambda g: (0, g, 0)),
            pl.BlockSpec((1, tiles, 2 * TILE), lambda g: (g, 0, 0)),
        ],
        out_specs=pl.BlockSpec((parts, GROUP, local_len), lambda g: (0, g, 0)),
        out_shape=jax.ShapeDtypeStruct(data.shape, jnp.bfloat16),
        scratch_shapes=[
            pltpu.VMEM((2 * rows, BLOCK), jnp.bfloat16),
            pltpu.VMEM((tiles, TILE, TILE), jnp.bfloat16),
            pltpu.VMEM((rows, BLOCK), jnp.float32),
        ],
        compiler_params=pltpu.CompilerParams(vmem_limit_bytes=32 * 1024 * 1024),
        cost_estimate=pl.CostEstimate(
            flops=2 * groups * blocks * rows * BLOCK * BLOCK,
            bytes_accessed=4 * parts * channels * local_len,
            transcendentals=0,
        ),
    )(data, lags)


def on_device(query_in, key_in, value_in, short_weight, long_filter, skip_gain, w_out):
    local_len, width = query_in.shape
    parts = lax.axis_size("seq")
    slabs = lax.axis_size("chan")
    chan = lax.axis_index("chan")
    columns = w_out.shape[1]
    chunk = 128
    gathered = [
        lax.all_gather(w_out[:, at : at + chunk], "seq", axis=1, tiled=True)
        for at in range(0, columns, chunk)
    ]

    filt = lax.all_to_all(
        long_filter.astype(jnp.bfloat16).reshape(parts, -1, local_len),
        "seq",
        split_axis=0,
        concat_axis=0,
        tiled=True,
    )
    groups = filt.shape[1]
    filt = jnp.transpose(filt, (1, 0, 2)).reshape(groups, -1, TILE).astype(jnp.float32)
    now = jnp.pad(filt, ((0, 0), (1, 0), (0, 0)))
    before = jnp.pad(filt[:, :-1], ((0, 0), (2, 0), (0, 0)))
    lags = jnp.concatenate([before, now], axis=2)

    ends = jnp.stack([a[local_len - (KW - 1) :] for a in (query_in, key_in, value_in)])
    border = lax.ppermute(ends, "seq", [(i, i + 1) for i in range(parts - 1)])
    border = jnp.pad(border.astype(jnp.float32), ((0, 0), (8 - (KW - 1), 0), (0, 0)))
    query_conv, gated = front(query_in, key_in, value_in, border, short_weight)
    moved = lax.all_to_all(
        gated.reshape(parts, -1, local_len), "seq", split_axis=0, concat_axis=0, tiled=True
    )
    conv = long_conv(moved, lags)
    conv = lax.all_to_all(conv, "seq", split_axis=0, concat_axis=0, tiled=True)
    conv = conv.reshape(width, local_len)
    mixed = (
        query_conv.astype(jnp.float32)
        * (conv.astype(jnp.float32) + skip_gain[:, None] * gated.astype(jnp.float32))
    ).astype(jnp.bfloat16)
    mixed = lax.optimization_barrier(mixed.T)

    outs = []
    for weights in gathered:
        terms = jnp.dot(mixed, weights, preferred_element_type=jnp.float32).astype(jnp.bfloat16)
        if slabs == 2:
            own = terms.shape[1] // 2
            sent = lax.dynamic_slice_in_dim(terms, (1 - chan) * own, own, 1)
            kept = lax.dynamic_slice_in_dim(terms, chan * own, own, 1)
            got = lax.ppermute(sent, "chan", [(0, 1), (1, 0)])
            summed = (kept.astype(jnp.float32) + got.astype(jnp.float32)).astype(jnp.bfloat16)
        else:
            summed = lax.psum_scatter(terms, "chan", scatter_dimension=1, tiled=True)
        outs.append(summed.reshape(local_len, -1, chunk))
    return jnp.stack(outs, axis=2).reshape(local_len, -1)


def solution(mesh):
    placed = (
        P("seq", "chan"),
        P("seq", "chan"),
        P("seq", "chan"),
        P(None, None, "chan"),
        P("chan", "seq"),
        P("chan"),
        P("chan", "seq"),
    )
    return jax.shard_map(
        on_device, mesh=mesh, in_specs=placed, out_specs=P("seq", "chan"), check_vma=False
    )
```

```python
import functools

import jax
import jax.numpy as jnp
from jax import lax
from jax.experimental import pallas as pl
from jax.experimental.pallas import tpu as pltpu
from jax.sharding import PartitionSpec as P

GROUP = 16
KW = 3
BLOCK = 256
TILE = 128
RUN = 8


def short_taps(x, border, taps):
    rows = x.shape[0]
    extended = jnp.concatenate([border, x.astype(jnp.float32)], axis=0)
    first = border.shape[0]
    total = taps[0:1] * extended[first:]
    for shift in range(1, KW):
        total = total + taps[shift : shift + 1] * extended[first - shift : first - shift + rows]
    return total


def front_kernel(q_ref, k_ref, v_ref, border_ref, taps_ref, query_ref, gated_ref):
    query = short_taps(q_ref[...], border_ref[0], taps_ref[0])
    key = short_taps(k_ref[...], border_ref[1], taps_ref[1])
    value = short_taps(v_ref[...], border_ref[2], taps_ref[2])
    query_ref[...] = query.T.astype(jnp.bfloat16)
    gated_ref[...] = (key * value).T.astype(jnp.bfloat16)


def front(query_in, key_in, value_in, border, taps):
    rows, width = query_in.shape
    wide = min(width, 256)
    signal = pl.BlockSpec((rows, wide), lambda i: (0, i))
    turned = pl.BlockSpec((wide, rows), lambda i: (i, 0))
    return pl.pallas_call(
        front_kernel,
        grid=(width // wide,),
        in_specs=[
            signal,
            signal,
            signal,
            pl.BlockSpec((3, 8, wide), lambda i: (0, 0, i)),
            pl.BlockSpec((3, KW, wide), lambda i: (0, 0, i)),
        ],
        out_specs=[turned, turned],
        out_shape=[jax.ShapeDtypeStruct((width, rows), jnp.bfloat16)] * 2,
        compiler_params=pltpu.CompilerParams(vmem_limit_bytes=32 * 1024 * 1024),
        cost_estimate=pl.CostEstimate(
            flops=20 * rows * width, bytes_accessed=10 * rows * width, transcendentals=0
        ),
    )(query_in, key_in, value_in, border, taps)


def conv_kernel(parts, blocks, data_ref, lags_ref, out_ref, held, toeplitz, total):
    local_len = data_ref.shape[2]
    per = local_len // BLOCK
    rows = blocks * GROUP
    held[0:rows, :] = jnp.zeros((rows, BLOCK), held.dtype)
    for part in range(parts):
        for piece in range(per):
            at = rows + (part * per + piece) * GROUP
            held[at : at + GROUP, :] = data_ref[part, :, piece * BLOCK : (piece + 1) * BLOCK]

    toeplitz[0] = jnp.zeros((TILE, TILE), toeplitz.dtype)
    wide = (RUN + 1) * TILE

    def build(step, carry):
        line = jnp.broadcast_to(lags_ref[0, pl.ds(step, 1), :], (TILE, wide))
        turned = pltpu.roll(line, 0, 1, stride=1, stride_axis=0).astype(jnp.bfloat16)
        for tile in range(RUN):
            at = (tile + 1) * TILE
            toeplitz[pl.ds(step * RUN + tile + 1, 1)] = turned[:, at : at + TILE][None]
        return carry

    lax.fori_loop(0, lags_ref.shape[1], build, 0)
    total[...] = jnp.zeros_like(total)
    half = rows // 2

    def weights(k):
        now = toeplitz[2 * k + 1]
        return jnp.concatenate(
            [
                jnp.concatenate([now, toeplitz[2 * k + 2]], axis=1),
                jnp.concatenate([toeplitz[2 * k], now], axis=1),
            ],
            axis=0,
        )

    def lagged(first, count, k):
        signal = [
            held[pl.ds(pl.multiple_of(first - lag * GROUP, GROUP), count), :] for lag in (k, k + 1)
        ]
        return jnp.dot(
            jnp.concatenate(signal, axis=1),
            jnp.concatenate([weights(k), weights(k + 1)], axis=0),
            preferred_element_type=jnp.float32,
        )

    def near(step, carry):
        total[...] += lagged(rows, rows, 2 * step)
        return carry

    def far(step, carry):
        total[half:, :] += lagged(rows + half, half, 2 * step)
        return carry

    lax.fori_loop(0, blocks // 4, near, 0)
    lax.fori_loop(blocks // 4, blocks // 2, far, 0)
    for part in range(parts):
        for piece in range(per):
            at = (part * per + piece) * GROUP
            out_ref[part, :, piece * BLOCK : (piece + 1) * BLOCK] = total[
                at : at + GROUP, :
            ].astype(jnp.bfloat16)


def long_conv(data, lags):
    parts, channels, local_len = data.shape
    groups, runs, wide = lags.shape
    tiles = runs * RUN + 1
    blocks = parts * local_len // BLOCK
    rows = blocks * GROUP
    return pl.pallas_call(
        functools.partial(conv_kernel, parts, blocks),
        grid=(groups,),
        in_specs=[
            pl.BlockSpec((parts, GROUP, local_len), lambda g: (0, g, 0)),
            pl.BlockSpec((1, runs, wide), lambda g: (g, 0, 0)),
        ],
        out_specs=pl.BlockSpec((parts, GROUP, local_len), lambda g: (0, g, 0)),
        out_shape=jax.ShapeDtypeStruct(data.shape, jnp.bfloat16),
        scratch_shapes=[
            pltpu.VMEM((2 * rows, BLOCK), jnp.bfloat16),
            pltpu.VMEM((tiles, TILE, TILE), jnp.bfloat16),
            pltpu.VMEM((rows, BLOCK), jnp.float32),
        ],
        compiler_params=pltpu.CompilerParams(vmem_limit_bytes=32 * 1024 * 1024),
        cost_estimate=pl.CostEstimate(
            flops=2 * groups * blocks * rows * BLOCK * BLOCK,
            bytes_accessed=4 * parts * channels * local_len,
            transcendentals=0,
        ),
    )(data, lags)


def join_kernel(shape, chunk, core_ref, *refs):
    chunks, addends, pairs = shape
    out_ref = refs[-1]

    def place(core):
        for at in range(chunks):
            for side in range(2):
                first = (at * 2 + side) * addends
                for pair in range(pairs):
                    cols = slice(pair * chunk, (pair + 1) * chunk)
                    total = refs[first][:, cols]
                    if addends == 2:
                        more = refs[first + 1][:, cols].astype(jnp.float32)
                        total = (total.astype(jnp.float32) + more).astype(jnp.bfloat16)
                    owner = pair * 2 + (core + side) % 2
                    to = (owner * chunks + at) * chunk
                    out_ref[:, to : to + chunk] = total

    for core in range(2):
        pl.when(core_ref[0] == core)(functools.partial(place, core))


def join(core, pieces, local_len, chunk):
    flat = [array for both in pieces for side in both for array in side]
    addends = len(pieces[0][0])
    wide = flat[0].shape[1]
    rows = 128
    total = 2 * len(pieces) * wide
    return pl.pallas_call(
        functools.partial(join_kernel, (len(pieces), addends, wide // chunk), chunk),
        grid=(local_len // rows,),
        in_specs=[pl.BlockSpec(memory_space=pltpu.SMEM)]
        + [pl.BlockSpec((rows, wide), lambda i: (i, 0))] * len(flat),
        out_specs=pl.BlockSpec((rows, total), lambda i: (i, 0)),
        out_shape=jax.ShapeDtypeStruct((local_len, total), jnp.bfloat16),
        compiler_params=pltpu.CompilerParams(vmem_limit_bytes=32 * 1024 * 1024),
    )(core, *flat)


def on_device(query_in, key_in, value_in, short_weight, long_filter, skip_gain, w_out):
    local_len, width = query_in.shape
    parts = lax.axis_size("seq")
    slabs = lax.axis_size("chan")
    chan = lax.axis_index("chan")
    columns = w_out.shape[1]
    chunk = 128
    same_core = [list(range(core, parts, 2)) for core in range(2)]
    gathered = [
        lax.all_gather(
            w_out[:, at : at + chunk], "seq", axis=1, tiled=True, axis_index_groups=same_core
        )
        for at in range(0, columns, chunk)
    ]

    filt = lax.all_to_all(
        long_filter.astype(jnp.bfloat16).reshape(parts, -1, local_len),
        "seq",
        split_axis=0,
        concat_axis=0,
        tiled=True,
    )
    groups = filt.shape[1]
    filt = jnp.transpose(filt, (1, 0, 2)).reshape(groups, -1, RUN * TILE).astype(jnp.float32)
    before = jnp.pad(filt[:, :-1, -TILE:], ((0, 0), (1, 0), (0, 0)))
    lags = jnp.concatenate([before, filt], axis=2)

    ends = jnp.stack([a[local_len - (KW - 1) :] for a in (query_in, key_in, value_in)])
    border = lax.ppermute(ends, "seq", [(i, i + 1) for i in range(parts - 1)])
    border = jnp.pad(border.astype(jnp.float32), ((0, 0), (8 - (KW - 1), 0), (0, 0)))
    query_conv, gated = front(query_in, key_in, value_in, border, short_weight)
    moved = lax.all_to_all(
        gated.reshape(parts, -1, local_len), "seq", split_axis=0, concat_axis=0, tiled=True
    )
    conv = long_conv(moved, lags)
    conv = lax.all_to_all(conv, "seq", split_axis=0, concat_axis=0, tiled=True)
    conv = conv.reshape(width, local_len)
    mixed = (
        query_conv.astype(jnp.float32)
        * (conv.astype(jnp.float32) + skip_gain[:, None] * gated.astype(jnp.float32))
    ).astype(jnp.bfloat16)
    mixed = lax.optimization_barrier(mixed.T)

    def slab_sum(weights):
        terms = jnp.dot(mixed, weights, preferred_element_type=jnp.float32).astype(jnp.bfloat16)
        if slabs != 2:
            return [lax.psum_scatter(terms, "chan", scatter_dimension=1, tiled=True)]
        own = terms.shape[1] // 2
        sent = lax.dynamic_slice_in_dim(terms, (1 - chan) * own, own, 1)
        kept = lax.dynamic_slice_in_dim(terms, chan * own, own, 1)
        return [kept, lax.ppermute(sent, "chan", [(0, 1), (1, 0)])]

    pairs = [(i, i ^ 1) for i in range(parts)]
    pieces = []
    for weights in gathered:
        others = lax.ppermute(weights, "seq", pairs)
        pieces.append([slab_sum(weights), slab_sum(others)])
    core = (lax.axis_index("seq") % 2).astype(jnp.int32).reshape(1)
    return join(core, pieces, local_len, chunk)


def solution(mesh):
    placed = (
        P("seq", "chan"),
        P("seq", "chan"),
        P("seq", "chan"),
        P(None, None, "chan"),
        P("chan", "seq"),
        P("chan"),
        P("chan", "seq"),
    )
    return jax.shard_map(
        on_device, mesh=mesh, in_specs=placed, out_specs=P("seq", "chan"), check_vma=False
    )
```

```python
import functools

import jax
import jax.numpy as jnp
from jax import lax
from jax.experimental import pallas as pl
from jax.experimental.pallas import tpu as pltpu
from jax.sharding import PartitionSpec as P

GROUP = 16
KW = 3
BLOCK = 256
TILE = 128
RUN = 8


def short_taps(x, border, taps):
    rows = x.shape[0]
    extended = jnp.concatenate([border, x.astype(jnp.float32)], axis=0)
    first = border.shape[0]
    total = taps[0:1] * extended[first:]
    for shift in range(1, KW):
        total = total + taps[shift : shift + 1] * extended[first - shift : first - shift + rows]
    return total


def front_kernel(q_ref, k_ref, v_ref, border_ref, taps_ref, query_ref, gated_ref):
    query = short_taps(q_ref[...], border_ref[0], taps_ref[0])
    key = short_taps(k_ref[...], border_ref[1], taps_ref[1])
    value = short_taps(v_ref[...], border_ref[2], taps_ref[2])
    query_ref[...] = query.T.astype(jnp.bfloat16)
    gated_ref[...] = (key * value).T.astype(jnp.bfloat16)


def front(query_in, key_in, value_in, border, taps):
    rows, width = query_in.shape
    wide = min(width, 256)
    signal = pl.BlockSpec((rows, wide), lambda i: (0, i))
    turned = pl.BlockSpec((wide, rows), lambda i: (i, 0))
    return pl.pallas_call(
        front_kernel,
        grid=(width // wide,),
        in_specs=[
            signal,
            signal,
            signal,
            pl.BlockSpec((3, 8, wide), lambda i: (0, 0, i)),
            pl.BlockSpec((3, KW, wide), lambda i: (0, 0, i)),
        ],
        out_specs=[turned, turned],
        out_shape=[jax.ShapeDtypeStruct((width, rows), jnp.bfloat16)] * 2,
        compiler_params=pltpu.CompilerParams(vmem_limit_bytes=32 * 1024 * 1024),
        cost_estimate=pl.CostEstimate(
            flops=20 * rows * width, bytes_accessed=10 * rows * width, transcendentals=0
        ),
    )(query_in, key_in, value_in, border, taps)


def conv_kernel(parts, blocks, data_ref, lags_ref, out_ref, held, toeplitz, total):
    local_len = data_ref.shape[2]
    per = local_len // BLOCK
    rows = blocks * GROUP
    held[0:rows, :] = jnp.zeros((rows, BLOCK), held.dtype)
    for part in range(parts):
        for piece in range(per):
            at = rows + (part * per + piece) * GROUP
            held[at : at + GROUP, :] = data_ref[part, :, piece * BLOCK : (piece + 1) * BLOCK]

    toeplitz[0] = jnp.zeros((TILE, TILE), toeplitz.dtype)
    wide = (RUN + 1) * TILE

    def build(step, carry):
        line = jnp.broadcast_to(lags_ref[0, pl.ds(step, 1), :], (TILE, wide))
        turned = pltpu.roll(line, 0, 1, stride=1, stride_axis=0).astype(jnp.bfloat16)
        for tile in range(RUN):
            at = (tile + 1) * TILE
            toeplitz[pl.ds(step * RUN + tile + 1, 1)] = turned[:, at : at + TILE][None]
        return carry

    lax.fori_loop(0, lags_ref.shape[1], build, 0)
    total[...] = jnp.zeros_like(total)
    half = rows // 2

    def weights(k):
        now = toeplitz[2 * k + 1]
        return jnp.concatenate(
            [
                jnp.concatenate([now, toeplitz[2 * k + 2]], axis=1),
                jnp.concatenate([toeplitz[2 * k], now], axis=1),
            ],
            axis=0,
        )

    def lagged(first, count, k):
        signal = [
            held[pl.ds(pl.multiple_of(first - lag * GROUP, GROUP), count), :] for lag in (k, k + 1)
        ]
        return jnp.dot(
            jnp.concatenate(signal, axis=1),
            jnp.concatenate([weights(k), weights(k + 1)], axis=0),
            preferred_element_type=jnp.float32,
        )

    def near(step, carry):
        total[...] += lagged(rows, rows, 2 * step)
        return carry

    def far(step, carry):
        total[half:, :] += lagged(rows + half, half, 2 * step)
        return carry

    lax.fori_loop(0, blocks // 4, near, 0)
    lax.fori_loop(blocks // 4, blocks // 2, far, 0)
    for part in range(parts):
        for piece in range(per):
            at = (part * per + piece) * GROUP
            out_ref[part, :, piece * BLOCK : (piece + 1) * BLOCK] = total[
                at : at + GROUP, :
            ].astype(jnp.bfloat16)


def long_conv(data, lags):
    parts, channels, local_len = data.shape
    groups, runs, wide = lags.shape
    tiles = runs * RUN + 1
    blocks = parts * local_len // BLOCK
    rows = blocks * GROUP
    return pl.pallas_call(
        functools.partial(conv_kernel, parts, blocks),
        grid=(groups,),
        in_specs=[
            pl.BlockSpec((parts, GROUP, local_len), lambda g: (0, g, 0)),
            pl.BlockSpec((1, runs, wide), lambda g: (g, 0, 0)),
        ],
        out_specs=pl.BlockSpec((parts, GROUP, local_len), lambda g: (0, g, 0)),
        out_shape=jax.ShapeDtypeStruct(data.shape, jnp.bfloat16),
        scratch_shapes=[
            pltpu.VMEM((2 * rows, BLOCK), jnp.bfloat16),
            pltpu.VMEM((tiles, TILE, TILE), jnp.bfloat16),
            pltpu.VMEM((rows, BLOCK), jnp.float32),
        ],
        compiler_params=pltpu.CompilerParams(vmem_limit_bytes=32 * 1024 * 1024),
        cost_estimate=pl.CostEstimate(
            flops=2 * groups * blocks * rows * BLOCK * BLOCK,
            bytes_accessed=4 * parts * channels * local_len,
            transcendentals=0,
        ),
    )(data, lags)


def join_kernel(shape, chunk, *refs):
    chunks, addends, owners = shape
    out_ref = refs[-1]
    for at in range(chunks):
        for owner in range(owners):
            cols = slice(owner * chunk, (owner + 1) * chunk)
            total = refs[at * addends][:, cols]
            if addends == 2:
                more = refs[at * addends + 1][:, cols].astype(jnp.float32)
                total = (total.astype(jnp.float32) + more).astype(jnp.bfloat16)
            to = (owner * chunks + at) * chunk
            out_ref[:, to : to + chunk] = total


def join(pieces, local_len, chunk):
    flat = [array for piece in pieces for array in piece]
    wide = flat[0].shape[1]
    rows = 128
    total = len(pieces) * wide
    return pl.pallas_call(
        functools.partial(join_kernel, (len(pieces), len(pieces[0]), wide // chunk), chunk),
        grid=(local_len // rows,),
        in_specs=[pl.BlockSpec((rows, wide), lambda i: (i, 0))] * len(flat),
        out_specs=pl.BlockSpec((rows, total), lambda i: (i, 0)),
        out_shape=jax.ShapeDtypeStruct((local_len, total), jnp.bfloat16),
        compiler_params=pltpu.CompilerParams(vmem_limit_bytes=32 * 1024 * 1024),
    )(*flat)


def on_device(query_in, key_in, value_in, short_weight, long_filter, skip_gain, w_out):
    local_len, width = query_in.shape
    parts = lax.axis_size("seq")
    slabs = lax.axis_size("chan")
    chan = lax.axis_index("chan")
    columns = w_out.shape[1]
    chunk = 128
    gathered = [
        lax.all_gather(w_out[:, at : at + chunk], "seq", axis=1, tiled=True)
        for at in range(0, columns, chunk)
    ]

    filt = lax.all_to_all(
        long_filter.astype(jnp.bfloat16).reshape(parts, -1, local_len),
        "seq",
        split_axis=0,
        concat_axis=0,
        tiled=True,
    )
    groups = filt.shape[1]
    filt = jnp.transpose(filt, (1, 0, 2)).reshape(groups, -1, RUN * TILE).astype(jnp.float32)
    before = jnp.pad(filt[:, :-1, -TILE:], ((0, 0), (1, 0), (0, 0)))
    lags = jnp.concatenate([before, filt], axis=2)

    ends = jnp.stack([a[local_len - (KW - 1) :] for a in (query_in, key_in, value_in)])
    border = lax.ppermute(ends, "seq", [(i, i + 1) for i in range(parts - 1)])
    border = jnp.pad(border.astype(jnp.float32), ((0, 0), (8 - (KW - 1), 0), (0, 0)))
    query_conv, gated = front(query_in, key_in, value_in, border, short_weight)
    moved = lax.all_to_all(
        gated.reshape(parts, -1, local_len), "seq", split_axis=0, concat_axis=0, tiled=True
    )
    conv = long_conv(moved, lags)
    conv = lax.all_to_all(conv, "seq", split_axis=0, concat_axis=0, tiled=True)
    conv = conv.reshape(width, local_len)
    mixed = (
        query_conv.astype(jnp.float32)
        * (conv.astype(jnp.float32) + skip_gain[:, None] * gated.astype(jnp.float32))
    ).astype(jnp.bfloat16)
    mixed = lax.optimization_barrier(mixed.T)

    def slab_sum(weights):
        terms = jnp.dot(mixed, weights, preferred_element_type=jnp.float32).astype(jnp.bfloat16)
        if slabs != 2:
            return [lax.psum_scatter(terms, "chan", scatter_dimension=1, tiled=True)]
        own = terms.shape[1] // 2
        sent = lax.dynamic_slice_in_dim(terms, (1 - chan) * own, own, 1)
        kept = lax.dynamic_slice_in_dim(terms, chan * own, own, 1)
        return [kept, lax.ppermute(sent, "chan", [(0, 1), (1, 0)])]

    return join([slab_sum(weights) for weights in gathered], local_len, chunk)


def solution(mesh):
    placed = (
        P("seq", "chan"),
        P("seq", "chan"),
        P("seq", "chan"),
        P(None, None, "chan"),
        P("chan", "seq"),
        P("chan"),
        P("chan", "seq"),
    )
    return jax.shard_map(
        on_device, mesh=mesh, in_specs=placed, out_specs=P("seq", "chan"), check_vma=False
    )
```
